256 devices in a mesh: kpool: 64 (over y, z_lo, x, core), band: 4 (over z_hi).
Axes of the slice: x: 4, y: 4, z: 8 (z_hi: 4, z_lo: 2; z = z_hi * 2 + z_lo), core: 2. Of those that a mesh axis runs over, the one named last changes fastest.
Arguments:
- psi: bfloat16 [64, 2, 4, 48, 2304], P('kpool', None, 'band'), may hold values from -6 to 6
- kpoint_of_pool: int32 [64], replicated, may hold values from 0 to 63, each once
Outputs:
- exchange: float32 [64, 2, 4, 48, 2304], P('kpool', None, 'band')
The draws below stay inside these ranges and needn't reach their ends.
Inputs may be any that keep to these rules, and one draw needn't show every extreme that they name: `kpoint_of_pool`: each value appears once.
All inputs are finite; a program needn't handle non-finite values.
Results may differ from the reference program's by a relative error of at most 0.0003.
Values may be sent and summed in bfloat16 or wider, within the bound.
No kernel may reach another device: no remote copies, remote signals or barrier semaphores. Data moves between devices by JAX's collectives and lax.ppermute only.
A program may use at most 64 MiB of HBM per device.

```python
import jax
import jax.numpy as jnp
from jax import lax

GRID = 48
KMESH = 4
ROUNDS = 1
NK = 64
BLOCK = 4


def levels(stream_key, shape, split, smallest, top_value):
    def one(axis_at, parts):
        draws = jax.random.uniform(jax.random.fold_in(jax.random.fold_in(stream_key, 6), axis_at), (parts,), jnp.float32, smallest / len(split), top_value / len(split))
        return jnp.repeat(jnp.exp(draws), shape[axis_at] // parts).reshape((-1,) + (1,) * (len(shape) - axis_at - 1))

    loudness = one(*split[0])
    for cut in split[1:]:
        loudness = loudness * one(*cut)
    return loudness


def normal_values(stream_key, extent, deviation, limit, shards=(), kind=jnp.bfloat16):
    values = jax.random.normal(stream_key, extent, jnp.float32) * deviation
    if len(shards) > 0:
        values = levels(stream_key, extent, shards, -0.22, 0.18) * values
    return jnp.clip(values, min=-limit, max=limit).astype(kind)


def setup_inputs(seed: int = 0) -> dict:
    splits = jax.random.split(jax.random.key(seed), 3)
    psi = normal_values(splits[0], (NK, 2, BLOCK, GRID, GRID * GRID), 1.0, 6.0, ((0, 64), (2, 4)))
    kpoint_of_pool = jax.random.permutation(splits[1], NK).astype(jnp.int32)
    return {"psi": psi, "kpoint_of_pool": kpoint_of_pool}


def kpoint_coords(labels):
    first = labels % KMESH
    second = (labels // KMESH) % KMESH
    third = labels // (KMESH * KMESH)
    return jnp.stack([first, second, third], axis=1).astype(jnp.float32) / KMESH


def coulomb(offset):
    index = jnp.arange(GRID, dtype=jnp.int32)
    freq = jnp.where(index < GRID // 2, index, index - GRID).astype(jnp.float32)
    edge = index == GRID // 2
    along_x = (offset[0] + freq) ** 2
    along_y = (offset[1] + freq) ** 2
    along_z = (offset[2] + freq) ** 2
    squared = along_x[:, None, None] + along_y[None, :, None] + along_z[None, None, :]
    cutoff = edge[:, None, None] | edge[None, :, None] | edge[None, None, :]
    safe = jnp.where(cutoff, 1.0, squared)
    amplitude = GRID ** 1.5 / 16.0
    return jnp.where(cutoff, 0.0, amplitude / safe)


def reference(psi, kpoint_of_pool):
    orbitals = lax.complex(psi[:, 0].astype(jnp.float32), psi[:, 1].astype(jnp.float32))
    orbitals = orbitals.reshape(NK, BLOCK, GRID, GRID, GRID)
    coords = kpoint_coords(kpoint_of_pool)
    weight = -(2.0 * ROUNDS * BLOCK) ** -0.5
    npoints = GRID * GRID * GRID

    def one_pool(pool):
        own = orbitals[pool]
        total = jnp.zeros_like(own)
        for turn in range(1, ROUNDS + 1):
            for direction in (1, -1):
                partner = (pool - direction * turn) % NK
                other = orbitals[partner]
                kernel = coulomb(coords[pool] - coords[partner])
                density = jnp.conj(other)[None] * own[:, None]
                spectrum = jnp.fft.fftn(density, axes=(2, 3, 4)) / npoints
                potential = jnp.fft.ifftn(spectrum * kernel, axes=(2, 3, 4)) * npoints
                total = total + jnp.sum(other[None] * potential, axis=1)
        total = total * weight
        return jnp.stack([jnp.real(total), jnp.imag(total)]).reshape(2, BLOCK, GRID, GRID * GRID)

    return lax.map(one_pool, jnp.arange(NK, dtype=jnp.int32))
```

```python
import functools
import numpy as np, ml_dtypes
import jax, jax.numpy as jnp
from jax import lax
from jax.experimental import pallas as pl
from jax.sharding import PartitionSpec as P
from jax.experimental.pallas import tpu as pltpu

UN = 24
U1 = 9
U4 = 6
G = 48
YZ = G * G
BF = jnp.bfloat16
F32 = jnp.float32

def split_np(t):
    hi = t.astype(np.float32).astype(ml_dtypes.bfloat16)
    lo = (t - hi.astype(np.float64)).astype(np.float32).astype(ml_dtypes.bfloat16)
    return hi, lo

def tables():
    i = np.arange(G)
    ang = 2 * np.pi * (np.outer(i, i) % G) / G
    c, s = np.cos(ang), np.sin(ang)
    z16 = np.zeros((G, 16))
    fx = np.concatenate([np.concatenate([c, z16, -s, z16], 1), np.concatenate([s, z16, c, z16], 1)], 0)
    hi, lo = split_np(fx)
    tb = np.concatenate([np.concatenate([hi, lo], 1), np.concatenate([hi, np.zeros_like(lo)], 1)], 0)
    def mid(sgn):
        a = np.concatenate([c, sgn * s], 0)
        h, l = split_np(a)
        return np.concatenate([h, h, l], 1)
    ix = np.concatenate([np.concatenate([c, z16, -s, z16], 1), np.concatenate([s, z16, c, z16], 1)], 0)
    h, l = split_np(ix)
    ti = np.concatenate([np.concatenate([h, h], 1), np.concatenate([l, np.zeros_like(l)], 1)], 0)
    return tb, mid(1.0), mid(-1.0), ti

def split(d):
    hi = d.astype(BF)
    return hi, (d - hi.astype(F32)).astype(BF)

def mid_pass(d, table):
    hi, lo = split(d)
    b = jnp.concatenate([hi, lo, hi], axis=0)
    r = jnp.dot(table, b, preferred_element_type=F32)
    out = []
    lane = lax.broadcasted_iota(jnp.int32, (G, 128), 1)
    sg = jnp.where(lane < 64, 1.0, -1.0).astype(F32)
    for k in range(2):
        cpart = r[:G, k * 128:(k + 1) * 128]
        spart = r[G:, k * 128:(k + 1) * 128]
        out.append(cpart + pltpu.roll(spart, 64, 1) * sg)
    return out

def kernel(stages, own_ref, oth_ref, v_ref, tb_ref, tf_ref, tv_ref, ti_ref, acc_in_ref, acc_ref, g1, g2, g3):
    f = pl.program_id(0)

    @pl.when(f == 0)
    def _():
        acc_ref[...] = acc_in_ref[...]

    if 1 in stages:
        @pl.loop(0, 9 // U1)
        def _(jj):
          for h in range(U1):
            sl = pl.ds(pl.multiple_of(jj * (256 * U1) + h * 256, 256), 256)
            pr, pi = own_ref[0, :, sl].astype(F32), own_ref[1, :, sl].astype(F32)
            qr, qi = oth_ref[0, 0, :, sl].astype(F32), oth_ref[0, 1, :, sl].astype(F32)
            dr = qr * pr + qi * pi
            di = qr * pi - qi * pr
            rh, rl = split(dr)
            ih, il = split(di)
            s = jnp.concatenate([rh, ih, rl, il], axis=0)
            r = lax.dot_general(s, tb_ref[...], (((0,), (0,)), ((), ())), preferred_element_type=F32)
            g1[sl, :] = r[:, :128] + r[:, 128:]
    if 2 in stages:
        @pl.loop(0, 24 // UN)
        def _(j):
            for h in range(UN):
                y = j * (2 * UN) + h * 2
                rows = [pl.ds(pl.multiple_of((y + k) * G, G), G) for k in range(2)]
                d = jnp.concatenate([g1[rows[0], :], g1[rows[1], :]], axis=1)
                o = mid_pass(d, tf_ref[...])
                for k in range(2):
                    g2[rows[k], :] = o[k]
    if 3 in stages:
        @pl.loop(0, 24 // UN)
        def _(j):
            for h in range(UN):
                z = j * (2 * UN) + h * 2
                d = jnp.concatenate([g2[pl.ds(z + k, G, stride=G), :] for k in range(2)], axis=1)
                o = mid_pass(d, tf_ref[...])
                d = jnp.concatenate([o[k] * v_ref[0, z + k] for k in range(2)], axis=1)
                o = mid_pass(d, tv_ref[...])
                for k in range(2):
                    g3[pl.ds(pl.multiple_of((z + k) * G, G), G), :] = o[k]
    if 4 in stages:
        @pl.loop(0, 6 // U4)
        def _(jj):
          for hh in range(U4):
            j = jj * U4 + hh
            parts = []
            for h in range(4):
                y = j * 8 + h * 2
                d = jnp.concatenate([g3[pl.ds(y + k, G, stride=G), :] for k in range(2)], axis=1)
                parts += mid_pass(d, tv_ref[...])
            d = jnp.concatenate(parts, axis=0)
            hi, lo = split(d)
            b = jnp.concatenate([hi, lo], axis=1)
            r = lax.dot_general(ti_ref[...], b, (((1,), (1,)), ((), ())), preferred_element_type=F32)
            w = r[:96] + r[96:]
            wr, wi = w[:G], w[G:]
            sl = pl.ds(pl.multiple_of(j * 384, 128), 384)
            qr, qi = oth_ref[0, 0, :, sl].astype(F32), oth_ref[0, 1, :, sl].astype(F32)
            acc_ref[0, :, sl] += qr * wr - qi * wi
            acc_ref[1, :, sl] += qr * wi + qi * wr

def convolve(own, others, v, acc, vmap, stages=(1, 2, 3, 4)):
    nf = others.shape[0]
    tb, tf, tv, ti = tables()
    full = lambda a: pl.BlockSpec(a.shape, lambda f: (0,) * a.ndim)
    return pl.pallas_call(
        functools.partial(kernel, stages),
        grid=(nf,),
        in_specs=[full(own), pl.BlockSpec((1, 2, G, YZ), lambda f: (f, 0, 0, 0)),
                  pl.BlockSpec((1, G, G, 128), lambda f: (vmap(f), 0, 0, 0)),
                  full(tb), full(tf), full(tv), full(ti), full(acc)],
        out_specs=full(acc),
        out_shape=jax.ShapeDtypeStruct(acc.shape, F32),
        scratch_shapes=[pltpu.VMEM((YZ, 128), F32)] * 3,
        compiler_params=pltpu.CompilerParams(vmem_limit_bytes=48 << 20),
    )(own, others, v, jnp.asarray(tb), jnp.asarray(tf), jnp.asarray(tv), jnp.asarray(ti), acc)

def coulomb_zyx(offset):
    index = jnp.arange(G, dtype=jnp.int32)
    freq = jnp.where(index < G // 2, index, index - G).astype(F32)
    lane = jnp.arange(128, dtype=jnp.int32) % 64
    fx = jnp.where(lane < G // 2, lane, lane - G).astype(F32)
    ex = (lane == G // 2) | (lane >= G)
    e = index == G // 2
    ax = (offset[0] + fx) ** 2
    ay = (offset[1] + freq) ** 2
    az = (offset[2] + freq) ** 2
    sq = ax[None, None, :] + ay[None, :, None] + az[:, None, None]
    cut = ex[None, None, :] | e[None, :, None] | e[:, None, None]
    safe = jnp.where(cut, 1.0, sq)
    return jnp.where(cut, 0.0, (G ** 1.5 / 16.0 / G ** 3) / safe)


def kpoint_coords(labels):
    first = labels % 4
    second = labels // 4 % 4
    third = labels // 16
    return jnp.stack([first, second, third], axis=1).astype(F32) / 4


def per_device(psi, kpoint_of_pool):
    own = psi[0, :, 0]
    pools = lax.axis_size("kpool")
    block = lax.axis_size("band")
    myself = lax.axis_index("kpool")
    coords = kpoint_coords(kpoint_of_pool)
    here = lax.dynamic_index_in_dim(coords, myself, 0, keepdims=False)
    weight = -((2.0 * block) ** (-0.5))
    whole = lax.all_gather(own, "band", axis=0)
    acc = jnp.zeros((2, G, YZ), F32)
    for direction in (1, -1):
        partner = (myself - direction) % pools
        there = lax.dynamic_index_in_dim(coords, partner, 0, keepdims=False)
        v = coulomb_zyx(here - there) * weight
        arrived = lax.ppermute(whole, "kpool", [(i, (i + direction) % pools) for i in range(pools)])
        acc = convolve(own, arrived, v[None], acc, lambda f: 0)
    return acc[None, :, None]


def solution(mesh):
    in_specs = (P("kpool", None, "band", None, None), P())
    out_specs = P("kpool", None, "band", None, None)
    return jax.shard_map(per_device, mesh=mesh, in_specs=in_specs, out_specs=out_specs, check_vma=False)
```

```python
import functools
import numpy as np, ml_dtypes
import jax, jax.numpy as jnp
from jax import lax
from jax.experimental import pallas as pl
from jax.sharding import PartitionSpec as P
from jax.experimental.pallas import tpu as pltpu

G = 48
YZ = G * G
BF = jnp.bfloat16
F32 = jnp.float32

def split_np(t):
    hi = t.astype(np.float32).astype(ml_dtypes.bfloat16)
    lo = (t - hi.astype(np.float64)).astype(np.float32).astype(ml_dtypes.bfloat16)
    return hi, lo

def tables():
    i = np.arange(G)
    ang = 2 * np.pi * (np.outer(i, i) % G) / G
    c, s = np.cos(ang), np.sin(ang)
    z16 = np.zeros((G, 16))
    fx = np.concatenate([np.concatenate([c, z16, -s, z16], 1), np.concatenate([s, z16, c, z16], 1)], 0)
    hi, lo = split_np(fx)
    tb = np.concatenate([np.concatenate([hi, lo], 1), np.concatenate([hi, np.zeros_like(lo)], 1)], 0)
    def mid(sgn):
        a = np.concatenate([c, sgn * s], 0)
        h, l = split_np(a)
        return np.concatenate([h, h, l], 1)
    ix = np.concatenate([np.concatenate([c, z16, -s, z16], 1), np.concatenate([s, z16, c, z16], 1)], 0)
    h, l = split_np(ix)
    ti = np.concatenate([np.concatenate([h, h], 1), np.concatenate([l, np.zeros_like(l)], 1)], 0)
    return tb, mid(1.0), mid(-1.0), ti

def split(d):
    hi = d.astype(BF)
    return hi, (d - hi.astype(F32)).astype(BF)

def mid_pass(d, table):
    hi, lo = split(d)
    b = jnp.concatenate([hi, lo, hi], axis=0)
    r = jnp.dot(table, b, preferred_element_type=F32)
    out = []
    lane = lax.broadcasted_iota(jnp.int32, (G, 128), 1)
    sg = jnp.where(lane < 64, 1.0, -1.0).astype(F32)
    for k in range(2):
        cpart = r[:G, k * 128:(k + 1) * 128]
        spart = r[G:, k * 128:(k + 1) * 128]
        out.append(cpart + pltpu.roll(spart, 64, 1) * sg)
    return out


def kernel(first, places, own_ref, *rest):
    count = 1 + max(at for at, _ in places)
    arrays, rest = rest[:count], rest[count:]
    fields = [arrays[at] if index is None else arrays[at].at[index] for at, index in places]
    (v_ref, tb_ref, tf_ref, tv_ref, ti_ref), rest = rest[:5], rest[5:]
    acc_in_ref = None if first else rest[0]
    acc_ref, cur, g1, g2, g3, gb = rest if first else rest[1:]
    f = pl.program_id(0)

    @pl.when(f == 0)
    def _():
        acc_ref[...] = jnp.zeros_like(acc_ref) if first else acc_in_ref[...]

    for at, field in enumerate(fields):

        @pl.when(f == at)
        def _():
            cur[...] = field[...]

    for j in range(9):
        sl = slice(j * 256, j * 256 + 256)
        pr, pi = own_ref[0, :, sl].astype(F32), own_ref[1, :, sl].astype(F32)
        qr, qi = cur[0, :, sl].astype(F32), cur[1, :, sl].astype(F32)
        rh, rl = split(qr * pr + qi * pi)
        ih, il = split(qr * pi - qi * pr)
        s = jnp.concatenate([rh, ih, rl, il], axis=0)
        r = lax.dot_general(s, tb_ref[...], (((0,), (0,)), ((), ())), preferred_element_type=F32)
        g1[sl, :] = r[:, :128] + r[:, 128:]
    for y in range(0, G, 2):
        rows = [slice((y + k) * G, (y + k + 1) * G) for k in range(2)]
        o = mid_pass(jnp.concatenate([g1[rows[k], :] for k in range(2)], axis=1), tf_ref[...])
        for k in range(2):
            g2[rows[k], :] = o[k]
    for z in range(0, G, 2):
        d = jnp.concatenate([g2[pl.ds(z + k, G, stride=G), :] for k in range(2)], axis=1)
        o = mid_pass(d, tf_ref[...])
        d = jnp.concatenate([o[k] * v_ref[0, z + k] for k in range(2)], axis=1)
        o = mid_pass(d, tv_ref[...])
        for k in range(2):
            g3[(z + k) * G:(z + k + 1) * G, :] = o[k]
    for y in range(0, G, 2):
        d = jnp.concatenate([g3[pl.ds(y + k, G, stride=G), :] for k in range(2)], axis=1)
        o = mid_pass(d, tv_ref[...])
        for k in range(2):
            rows = slice((y + k) * G, (y + k + 1) * G)
            gb[rows, :128], gb[rows, 128:] = split(o[k])
    for j in range(9):
        sl = slice(j * 256, j * 256 + 256)
        r = lax.dot_general(ti_ref[...], gb[sl, :], (((1,), (1,)), ((), ())), preferred_element_type=F32)
        w = r[:96] + r[96:]
        wr, wi = w[:G], w[G:]
        qr, qi = cur[0, :, sl].astype(F32), cur[1, :, sl].astype(F32)
        acc_ref[0, :, sl] += qr * wr - qi * wi
        acc_ref[1, :, sl] += qr * wi + qi * wr


def convolve(own, fields, sides, v, acc):
    constants = [jnp.asarray(t) for t in tables()]
    first = acc is None
    flat, places = [], []
    for field in fields:
        array, index = field if isinstance(field, tuple) else (field, None)
        known = [k for k, other in enumerate(flat) if other is array]
        places.append((known[0] if known else len(flat), index))
        if not known:
            flat.append(array)
    operands = [own, *flat, v, *constants] + ([] if first else [acc])
    full = lambda t: pl.BlockSpec(t.shape, lambda f: (0,) * t.ndim)
    specs = [full(t) for t in operands]
    step = sides[-1] - sides[0]
    specs[1 + len(flat)] = pl.BlockSpec((1, G, G, 128), lambda f: (sides[0] + f * step, 0, 0, 0))
    shape = jax.ShapeDtypeStruct((2, G, YZ), F32)
    return pl.pallas_call(
        functools.partial(kernel, first, tuple(places)),
        grid=(len(fields),),
        in_specs=specs,
        out_specs=full(shape),
        out_shape=shape,
        scratch_shapes=[pltpu.VMEM((2, G, YZ), BF)] + [pltpu.VMEM((YZ, 128), F32)] * 3 + [pltpu.VMEM((YZ, 256), BF)],
        compiler_params=pltpu.CompilerParams(vmem_limit_bytes=40 << 20),
        cost_estimate=pl.CostEstimate(flops=int(1e8), bytes_accessed=1 << 16, transcendentals=0),
    )(*operands)


def coulomb_zyx(offset):
    index = jnp.arange(G, dtype=jnp.int32)
    freq = jnp.where(index < G // 2, index, index - G).astype(F32)
    lane = jnp.arange(128, dtype=jnp.int32) % 64
    fx = jnp.where(lane < G // 2, lane, lane - G).astype(F32)
    ex = (lane == G // 2) | (lane >= G)
    e = index == G // 2
    ax = (offset[0] + fx) ** 2
    ay = (offset[1] + freq) ** 2
    az = (offset[2] + freq) ** 2
    sq = ax[None, None, :] + ay[None, :, None] + az[:, None, None]
    cut = ex[None, None, :] | e[None, :, None] | e[:, None, None]
    safe = jnp.where(cut, 1.0, sq)
    return jnp.where(cut, 0.0, (G ** 1.5 / 16.0 / G ** 3) / safe)


def kpoint_coords(labels):
    first = labels % 4
    second = labels // 4 % 4
    third = labels // 16
    return jnp.stack([first, second, third], axis=1).astype(F32) / 4


def band_hop(value, by):
    n = lax.axis_size("band")
    return lax.ppermute(value, "band", [(i, (i + by) % n) for i in range(n)])


def swap_chip(value):
    n = lax.axis_size("kpool")
    return lax.ppermute(value, "kpool", [(i, i ^ 1) for i in range(n)])


def swap_next(value):
    n = lax.axis_size("kpool")
    return lax.ppermute(value, "kpool", [(i, (i + 1 if i % 2 else i - 1) % n) for i in range(n)])


def per_device(psi, kpoint_of_pool):
    own = psi[0, :, 0]
    pools = lax.axis_size("kpool")
    block = lax.axis_size("band")
    myself = lax.axis_index("kpool")
    coords = kpoint_coords(kpoint_of_pool)
    at = lambda pool: lax.dynamic_index_in_dim(coords, pool % pools, 0, keepdims=False)
    weight = -((2.0 * block) ** (-0.5))
    odd = myself % 2
    inner = myself + 1 - 2 * odd
    outer = myself - 1 + 2 * odd
    v = jnp.stack([coulomb_zyx(at(myself) - at(s)) * weight for s in (inner, outer)])
    acc = None
    outer, inner = swap_next(own), swap_chip(own)
    up, down = band_hop(own, 1), band_hop(own, -1)
    acc = convolve(own, [inner], [0], v, None)
    up, down, acc = lax.optimization_barrier((up, down, acc))
    across = [band_hop(up[0], 1), band_hop(down[1], -1)]
    both = jnp.stack([up, down])
    inner, outer_both = swap_chip(both), swap_next(both)
    acc = convolve(own, [(inner, 0), (inner, 1)], [0, 0], v, acc)
    acc = convolve(own, [outer], [1], v, acc)
    across, acc = lax.optimization_barrier((across, acc))
    across = jnp.stack(across)
    inner, outer = swap_chip(across), swap_next(across)
    acc = convolve(own, [inner], [0], v, acc)
    acc = convolve(own, [(outer_both, 0), (outer_both, 1)], [1, 1], v, acc)
    acc = convolve(own, [outer], [1], v, acc)
    return acc[None, :, None]


def solution(mesh):
    in_specs = (P("kpool", None, "band", None, None), P())
    out_specs = P("kpool", None, "band", None, None)
    return jax.shard_map(per_device, mesh=mesh, in_specs=in_specs, out_specs=out_specs, check_vma=False)
```

```python
import functools
import numpy as np, ml_dtypes
import jax, jax.numpy as jnp
from jax import lax
from jax.experimental import pallas as pl
from jax.sharding import PartitionSpec as P
from jax.experimental.pallas import tpu as pltpu

G = 48
YZ = G * G
PITCH = 49
BF = jnp.bfloat16
F32 = jnp.float32

def split_np(t):
    hi = t.astype(np.float32).astype(ml_dtypes.bfloat16)
    lo = (t - hi.astype(np.float64)).astype(np.float32).astype(ml_dtypes.bfloat16)
    return hi, lo

def tables():
    i = np.arange(G)
    ang = 2 * np.pi * (np.outer(i, i) % G) / G
    c, s = np.cos(ang), np.sin(ang)
    z16 = np.zeros((G, 16))
    fx = np.concatenate([np.concatenate([c, z16, -s, z16], 1), np.concatenate([s, z16, c, z16], 1)], 0)
    hi, lo = split_np(fx)
    tb = np.concatenate([np.concatenate([hi, lo], 1), np.concatenate([hi, np.zeros_like(lo)], 1)], 0)
    def mid(sgn):
        a = np.concatenate([c, sgn * s], 0)
        h, l = split_np(a)
        return np.concatenate([h, h, l], 1)
    ix = np.concatenate([np.concatenate([c, z16, -s, z16], 1), np.concatenate([s, z16, c, z16], 1)], 0)
    h, l = split_np(ix)
    ti = np.concatenate([np.concatenate([h, h], 1), np.concatenate([l, np.zeros_like(l)], 1)], 0)
    return tb, mid(1.0), mid(-1.0), ti

def split(d):
    hi = d.astype(BF)
    return hi, (d - hi.astype(F32)).astype(BF)

def mid_pass(d, table):
    hi, lo = split(d)
    b = jnp.concatenate([hi, lo, hi], axis=0)
    r = jnp.dot(table, b, preferred_element_type=F32)
    out = []
    lane = lax.broadcasted_iota(jnp.int32, (G, 128), 1)
    sg = jnp.where(lane < 64, 1.0, -1.0).astype(F32)
    for k in range(2):
        cpart = r[:G, k * 128:(k + 1) * 128]
        spart = r[G:, k * 128:(k + 1) * 128]
        out.append(cpart + pltpu.roll(spart, 64, 1) * sg)
    return out


def kernel(first, places, own_ref, *rest):
    count = 1 + max(at for at, _ in places)
    arrays, rest = rest[:count], rest[count:]
    fields = [arrays[at] if index is None else arrays[at].at[index] for at, index in places]
    (v_ref, tb_ref, tf_ref, tv_ref, ti_ref), rest = rest[:5], rest[5:]
    acc_in_ref = None if first else rest[0]
    acc_ref, cur, g1, g2, g3, gb = rest if first else rest[1:]
    f = pl.program_id(0)

    @pl.when(f == 0)
    def _():
        acc_ref[...] = jnp.zeros_like(acc_ref) if first else acc_in_ref[...]

    for at, field in enumerate(fields):

        @pl.when(f == at)
        def _():
            cur[...] = field[...]

    for j in range(9):
        sl = slice(j * 256, j * 256 + 256)
        pr, pi = own_ref[0, :, sl].astype(F32), own_ref[1, :, sl].astype(F32)
        qr, qi = cur[0, :, sl].astype(F32), cur[1, :, sl].astype(F32)
        rh, rl = split(qr * pr + qi * pi)
        ih, il = split(qr * pi - qi * pr)
        s = jnp.concatenate([rh, ih, rl, il], axis=0)
        r = lax.dot_general(s, tb_ref[...], (((0,), (0,)), ((), ())), preferred_element_type=F32)
        g1[sl, :] = r[:, :128] + r[:, 128:]
    for y in range(0, G, 2):
        rows = [slice((y + k) * G, (y + k + 1) * G) for k in range(2)]
        o = mid_pass(jnp.concatenate([g1[rows[k], :] for k in range(2)], axis=1), tf_ref[...])
        for k in range(2):
            g2[(y + k) * PITCH:(y + k) * PITCH + G, :] = o[k]
    for z in range(0, G, 2):
        d = jnp.concatenate([g2[pl.ds(z + k, G, stride=PITCH), :] for k in range(2)], axis=1)
        o = mid_pass(d, tf_ref[...])
        d = jnp.concatenate([o[k] * v_ref[0, z + k] for k in range(2)], axis=1)
        o = mid_pass(d, tv_ref[...])
        for k in range(2):
            g3[(z + k) * PITCH:(z + k) * PITCH + G, :] = o[k]
    for y in range(0, G, 2):
        d = jnp.concatenate([g3[pl.ds(y + k, G, stride=PITCH), :] for k in range(2)], axis=1)
        o = mid_pass(d, tv_ref[...])
        for k in range(2):
            rows = slice((y + k) * G, (y + k + 1) * G)
            gb[rows, :128], gb[rows, 128:] = split(o[k])
    for j in range(9):
        sl = slice(j * 256, j * 256 + 256)
        r = lax.dot_general(ti_ref[...], gb[sl, :], (((1,), (1,)), ((), ())), preferred_element_type=F32)
        w = r[:96] + r[96:]
        wr, wi = w[:G], w[G:]
        qr, qi = cur[0, :, sl].astype(F32), cur[1, :, sl].astype(F32)
        acc_ref[0, :, sl] += qr * wr - qi * wi
        acc_ref[1, :, sl] += qr * wi + qi * wr


def convolve(own, fields, sides, v, acc):
    constants = [jnp.asarray(t) for t in tables()]
    first = acc is None
    flat, places = [], []
    for field in fields:
        array, index = field if isinstance(field, tuple) else (field, None)
        known = [k for k, other in enumerate(flat) if other is array]
        places.append((known[0] if known else len(flat), index))
        if not known:
            flat.append(array)
    operands = [own, *flat, v, *constants] + ([] if first else [acc])
    full = lambda t: pl.BlockSpec(t.shape, lambda f: (0,) * t.ndim)
    specs = [full(t) for t in operands]
    step = sides[-1] - sides[0]
    specs[1 + len(flat)] = pl.BlockSpec((1, G, G, 128), lambda f: (sides[0] + f * step, 0, 0, 0))
    shape = jax.ShapeDtypeStruct((2, G, YZ), F32)
    return pl.pallas_call(
        functools.partial(kernel, first, tuple(places)),
        grid=(len(fields),),
        in_specs=specs,
        out_specs=full(shape),
        out_shape=shape,
        scratch_shapes=[pltpu.VMEM((2, G, YZ), BF)] + [pltpu.VMEM((YZ, 128), F32)] + [pltpu.VMEM((G * PITCH + 8, 128), F32)] * 2 + [pltpu.VMEM((YZ, 256), BF)],
        compiler_params=pltpu.CompilerParams(vmem_limit_bytes=40 << 20),
        cost_estimate=pl.CostEstimate(flops=int(1e8), bytes_accessed=1 << 16, transcendentals=0),
    )(*operands)


def coulomb_zyx(offset):
    index = jnp.arange(G, dtype=jnp.int32)
    freq = jnp.where(index < G // 2, index, index - G).astype(F32)
    lane = jnp.arange(128, dtype=jnp.int32) % 64
    fx = jnp.where(lane < G // 2, lane, lane - G).astype(F32)
    ex = (lane == G // 2) | (lane >= G)
    e = index == G // 2
    ax = (offset[0] + fx) ** 2
    ay = (offset[1] + freq) ** 2
    az = (offset[2] + freq) ** 2
    sq = ax[None, None, :] + ay[None, :, None] + az[:, None, None]
    cut = ex[None, None, :] | e[None, :, None] | e[:, None, None]
    safe = jnp.where(cut, 1.0, sq)
    return jnp.where(cut, 0.0, (G ** 1.5 / 16.0 / G ** 3) / safe)


def kpoint_coords(labels):
    first = labels % 4
    second = labels // 4 % 4
    third = labels // 16
    return jnp.stack([first, second, third], axis=1).astype(F32) / 4


def band_hop(value, by):
    n = lax.axis_size("band")
    return lax.ppermute(value, "band", [(i, (i + by) % n) for i in range(n)])


def swap_chip(value):
    n = lax.axis_size("kpool")
    return lax.ppermute(value, "kpool", [(i, i ^ 1) for i in range(n)])


def swap_next(value):
    n = lax.axis_size("kpool")
    return lax.ppermute(value, "kpool", [(i, (i + 1 if i % 2 else i - 1) % n) for i in range(n)])


def per_device(psi, kpoint_of_pool):
    own = psi[0, :, 0]
    pools = lax.axis_size("kpool")
    block = lax.axis_size("band")
    myself = lax.axis_index("kpool")
    coords = kpoint_coords(kpoint_of_pool)
    at = lambda pool: lax.dynamic_index_in_dim(coords, pool % pools, 0, keepdims=False)
    weight = -((2.0 * block) ** (-0.5))
    odd = myself % 2
    inner = myself + 1 - 2 * odd
    outer = myself - 1 + 2 * odd
    v = jnp.stack([coulomb_zyx(at(myself) - at(s)) * weight for s in (inner, outer)])
    acc = None
    outer, inner = swap_next(own), swap_chip(own)
    up, down = band_hop(own, 1), band_hop(own, -1)
    acc = convolve(own, [inner], [0], v, None)
    up, acc = lax.optimization_barrier((up, acc))
    hop_up = band_hop(up[0], 1)
    down, acc = lax.optimization_barrier((down, acc))
    across = [hop_up, band_hop(down[1], -1)]
    both = jnp.stack([up, down])
    inner, outer_both = swap_chip(both), swap_next(both)
    acc = convolve(own, [(inner, 0), (inner, 1)], [0, 0], v, acc)
    acc = convolve(own, [outer], [1], v, acc)
    across, acc = lax.optimization_barrier((across, acc))
    across = jnp.stack(across)
    inner, outer = swap_chip(across), swap_next(across)
    acc = convolve(own, [inner], [0], v, acc)
    acc = convolve(own, [(outer_both, 0), (outer_both, 1)], [1, 1], v, acc)
    acc = convolve(own, [outer], [1], v, acc)
    return acc[None, :, None]


def solution(mesh):
    in_specs = (P("kpool", None, "band", None, None), P())
    out_specs = P("kpool", None, "band", None, None)
    return jax.shard_map(per_device, mesh=mesh, in_specs=in_specs, out_specs=out_specs, check_vma=False)
```

```python
import functools
import numpy as np, ml_dtypes
import jax, jax.numpy as jnp
from jax import lax
from jax.experimental import pallas as pl
from jax.sharding import PartitionSpec as P
from jax.experimental.pallas import tpu as pltpu

G = 48
YZ = G * G
PITCH = 49
BF = jnp.bfloat16
F32 = jnp.float32

def split_np(t):
    hi = t.astype(np.float32).astype(ml_dtypes.bfloat16)
    lo = (t - hi.astype(np.float64)).astype(np.float32).astype(ml_dtypes.bfloat16)
    return hi, lo

def tables():
    i = np.arange(G)
    ang = 2 * np.pi * (np.outer(i, i) % G) / G
    c, s = np.cos(ang), np.sin(ang)
    z16 = np.zeros((G, 16))
    fx = np.concatenate([np.concatenate([c, z16, -s, z16], 1), np.concatenate([s, z16, c, z16], 1)], 0)
    hi, lo = split_np(fx)
    tb = np.concatenate([np.concatenate([hi, lo], 1), np.concatenate([hi, np.zeros_like(lo)], 1)], 0)
    def mid(sgn):
        a = np.concatenate([c, sgn * s], 0)
        h, l = split_np(a)
        return np.concatenate([h, h, l], 1)
    ix = np.concatenate([np.concatenate([c, z16, -s, z16], 1), np.concatenate([s, z16, c, z16], 1)], 0)
    h, l = split_np(ix)
    ti = np.concatenate([np.concatenate([h, h], 1), np.concatenate([l, np.zeros_like(l)], 1)], 0)
    return tb, mid(1.0), mid(-1.0), ti

def split(d):
    hi = d.astype(BF)
    return hi, (d - hi.astype(F32)).astype(BF)

def mid_pass(d, table):
    hi, lo = split(d)
    b = jnp.concatenate([hi, lo, hi], axis=0)
    r = jnp.dot(table, b, preferred_element_type=F32)
    out = []
    lane = lax.broadcasted_iota(jnp.int32, (G, 128), 1)
    sg = jnp.where(lane < 64, 1.0, -1.0).astype(F32)
    for k in range(2):
        cpart = r[:G, k * 128:(k + 1) * 128]
        spart = r[G:, k * 128:(k + 1) * 128]
        out.append(cpart + pltpu.roll(spart, 64, 1) * sg)
    return out


def kernel(first, places, own_ref, *rest):
    count = 1 + max(at for at, _ in places)
    arrays, rest = rest[:count], rest[count:]
    fields = [arrays[at] if index is None else arrays[at].at[index] for at, index in places]
    (v_ref, tb_ref, tf_ref, tv_ref, ti_ref), rest = rest[:5], rest[5:]
    acc_in_ref = None if first else rest[0]
    acc_ref, cur, g1, g2, g3, gb = rest if first else rest[1:]
    f = pl.program_id(0)

    @pl.when(f == 0)
    def _():
        acc_ref[...] = jnp.zeros_like(acc_ref) if first else acc_in_ref[...]

    for at, field in enumerate(fields):

        @pl.when(f == at)
        def _():
            cur[...] = field[...]

    for j in range(9):
        sl = slice(j * 256, j * 256 + 256)
        pr, pi = own_ref[0, :, sl].astype(F32), own_ref[1, :, sl].astype(F32)
        qr, qi = cur[0, :, sl].astype(F32), cur[1, :, sl].astype(F32)
        rh, rl = split(qr * pr + qi * pi)
        ih, il = split(qr * pi - qi * pr)
        s = jnp.concatenate([rh, ih, rl, il], axis=0)
        r = lax.dot_general(s, tb_ref[...], (((0,), (0,)), ((), ())), preferred_element_type=F32)
        g1[sl, :] = r[:, :128] + r[:, 128:]
    for y in range(0, G, 2):
        rows = [slice((y + k) * G, (y + k + 1) * G) for k in range(2)]
        o = mid_pass(jnp.concatenate([g1[rows[k], :] for k in range(2)], axis=1), tf_ref[...])
        for k in range(2):
            g2[(y + k) * PITCH:(y + k) * PITCH + G, :] = o[k]
    for z in range(0, G, 2):
        d = jnp.concatenate([g2[pl.ds(z + k, G, stride=PITCH), :] for k in range(2)], axis=1)
        o = mid_pass(d, tf_ref[...])
        d = jnp.concatenate([o[k] * v_ref[0, z + k] for k in range(2)], axis=1)
        o = mid_pass(d, tv_ref[...])
        for k in range(2):
            g3[(z + k) * PITCH:(z + k) * PITCH + G, :] = o[k]
    for y in range(0, G, 2):
        d = jnp.concatenate([g3[pl.ds(y + k, G, stride=PITCH), :] for k in range(2)], axis=1)
        o = mid_pass(d, tv_ref[...])
        for k in range(2):
            rows = slice((y + k) * G, (y + k + 1) * G)
            gb[rows, :128], gb[rows, 128:] = split(o[k])
    for j in range(9):
        sl = slice(j * 256, j * 256 + 256)
        r = lax.dot_general(ti_ref[...], gb[sl, :], (((1,), (1,)), ((), ())), preferred_element_type=F32)
        w = r[:96] + r[96:]
        wr, wi = w[:G], w[G:]
        qr, qi = cur[0, :, sl].astype(F32), cur[1, :, sl].astype(F32)
        acc_ref[0, :, sl] += qr * wr - qi * wi
        acc_ref[1, :, sl] += qr * wi + qi * wr


def convolve(own, fields, sides, v, acc):
    constants = [jnp.asarray(t) for t in tables()]
    first = acc is None
    flat, places = [], []
    for field in fields:
        array, index = field if isinstance(field, tuple) else (field, None)
        known = [k for k, other in enumerate(flat) if other is array]
        places.append((known[0] if known else len(flat), index))
        if not known:
            flat.append(array)
    operands = [own, *flat, v, *constants] + ([] if first else [acc])
    full = lambda t: pl.BlockSpec(t.shape, lambda f: (0,) * t.ndim)
    specs = [full(t) for t in operands]
    step = sides[-1] - sides[0]
    specs[1 + len(flat)] = pl.BlockSpec((1, G, G, 128), lambda f: (sides[0] + f * step, 0, 0, 0))
    shape = jax.ShapeDtypeStruct((2, G, YZ), F32)
    return pl.pallas_call(
        functools.partial(kernel, first, tuple(places)),
        grid=(len(fields),),
        in_specs=specs,
        out_specs=full(shape),
        out_shape=shape,
        scratch_shapes=[pltpu.VMEM((2, G, YZ), BF)] + [pltpu.VMEM((YZ, 128), F32)] + [pltpu.VMEM((G * PITCH + 8, 128), F32)] * 2 + [pltpu.VMEM((YZ, 256), BF)],
        compiler_params=pltpu.CompilerParams(vmem_limit_bytes=40 << 20),
        cost_estimate=pl.CostEstimate(flops=int(1e8), bytes_accessed=1 << 16, transcendentals=0),
    )(*operands)


def coulomb_zyx(offset):
    index = jnp.arange(G, dtype=jnp.int32)
    freq = jnp.where(index < G // 2, index, index - G).astype(F32)
    lane = jnp.arange(128, dtype=jnp.int32) % 64
    fx = jnp.where(lane < G // 2, lane, lane - G).astype(F32)
    ex = (lane == G // 2) | (lane >= G)
    e = index == G // 2
    ax = (offset[0] + fx) ** 2
    ay = (offset[1] + freq) ** 2
    az = (offset[2] + freq) ** 2
    sq = ax[None, None, :] + ay[None, :, None] + az[:, None, None]
    cut = ex[None, None, :] | e[None, :, None] | e[:, None, None]
    safe = jnp.where(cut, 1.0, sq)
    return jnp.where(cut, 0.0, (G ** 1.5 / 16.0 / G ** 3) / safe)


def kpoint_coords(labels):
    first = labels % 4
    second = labels // 4 % 4
    third = labels // 16
    return jnp.stack([first, second, third], axis=1).astype(F32) / 4


def band_hop(value, by):
    n = lax.axis_size("band")
    return lax.ppermute(value, "band", [(i, (i + by) % n) for i in range(n)])


def swap_chip(value):
    n = lax.axis_size("kpool")
    return lax.ppermute(value, "kpool", [(i, i ^ 1) for i in range(n)])


def swap_next(value):
    n = lax.axis_size("kpool")
    return lax.ppermute(value, "kpool", [(i, (i + 1 if i % 2 else i - 1) % n) for i in range(n)])


def per_device(psi, kpoint_of_pool):
    own = psi[0, :, 0]
    pools = lax.axis_size("kpool")
    block = lax.axis_size("band")
    myself = lax.axis_index("kpool")
    coords = kpoint_coords(kpoint_of_pool)
    at = lambda pool: lax.dynamic_index_in_dim(coords, pool % pools, 0, keepdims=False)
    weight = -((2.0 * block) ** (-0.5))
    odd = myself % 2
    inner = myself + 1 - 2 * odd
    outer = myself - 1 + 2 * odd
    v = jnp.stack([coulomb_zyx(at(myself) - at(s)) * weight for s in (inner, outer)])
    acc = None
    outer, inner = swap_next(own), swap_chip(own)
    up, down = band_hop(own, 1), band_hop(own, -1)
    acc = convolve(own, [inner], [0], v, None)
    up, acc = lax.optimization_barrier((up, acc))
    hop_up, inner_up = band_hop(up[0], 1), swap_chip(up)
    down, acc = lax.optimization_barrier((down, acc))
    across = [hop_up, band_hop(down[1], -1)]
    both = jnp.stack([up, down])
    inner_down, outer_both = swap_chip(down), swap_next(both)
    acc = convolve(own, [inner_up, inner_down], [0, 0], v, acc)
    acc = convolve(own, [outer], [1], v, acc)
    across, acc = lax.optimization_barrier((across, acc))
    across = jnp.stack(across)
    inner, outer = swap_chip(across), swap_next(across)
    acc = convolve(own, [inner], [0], v, acc)
    acc = convolve(own, [(outer_both, 0), (outer_both, 1)], [1, 1], v, acc)
    acc = convolve(own, [outer], [1], v, acc)
    return acc[None, :, None]


def solution(mesh):
    in_specs = (P("kpool", None, "band", None, None), P())
    out_specs = P("kpool", None, "band", None, None)
    return jax.shard_map(per_device, mesh=mesh, in_specs=in_specs, out_specs=out_specs, check_vma=False)
```

```python
import functools
import numpy as np, ml_dtypes
import jax, jax.numpy as jnp
from jax import lax
from jax.experimental import pallas as pl
from jax.sharding import PartitionSpec as P
from jax.experimental.pallas import tpu as pltpu

G = 48
YZ = G * G
PITCH = 49
BF = jnp.bfloat16
F32 = jnp.float32

def split_np(t):
    hi = t.astype(np.float32).astype(ml_dtypes.bfloat16)
    lo = (t - hi.astype(np.float64)).astype(np.float32).astype(ml_dtypes.bfloat16)
    return hi, lo

def tables():
    i = np.arange(G)
    ang = 2 * np.pi * (np.outer(i, i) % G) / G
    c, s = np.cos(ang), np.sin(ang)
    z16 = np.zeros((G, 16))
    fx = np.concatenate([np.concatenate([c, z16, -s, z16], 1), np.concatenate([s, z16, c, z16], 1)], 0)
    hi, lo = split_np(fx)
    tb = np.concatenate([np.concatenate([hi, lo], 1), np.concatenate([hi, np.zeros_like(lo)], 1)], 0)
    def mid(sgn):
        a = np.concatenate([c, sgn * s], 0)
        h, l = split_np(a)
        return np.concatenate([h, h, l], 1)
    ix = np.concatenate([np.concatenate([c, z16, -s, z16], 1), np.concatenate([s, z16, c, z16], 1)], 0)
    h, l = split_np(ix)
    ti = np.concatenate([np.concatenate([h, h], 1), np.concatenate([l, np.zeros_like(l)], 1)], 0)
    return tb, mid(1.0), mid(-1.0), ti

def split(d):
    hi = d.astype(BF)
    return hi, (d - hi.astype(F32)).astype(BF)

def mid_pass(d, table):
    hi, lo = split(d)
    b = jnp.concatenate([hi, lo, hi], axis=0)
    r = jnp.dot(table, b, preferred_element_type=F32)
    out = []
    lane = lax.broadcasted_iota(jnp.int32, (G, 128), 1)
    sg = jnp.where(lane < 64, 1.0, -1.0).astype(F32)
    for k in range(2):
        cpart = r[:G, k * 128:(k + 1) * 128]
        spart = r[G:, k * 128:(k + 1) * 128]
        out.append(cpart + pltpu.roll(spart, 64, 1) * sg)
    return out


def kernel(first, places, own_ref, *rest):
    count = 1 + max(at for at, _ in places)
    arrays, rest = rest[:count], rest[count:]
    fields = [arrays[at] if index is None else arrays[at].at[index] for at, index in places]
    (v_ref, tb_ref, tf_ref, tv_ref, ti_ref), rest = rest[:5], rest[5:]
    acc_in_ref = None if first else rest[0]
    acc_ref, cur, g1, g2, g3, gb = rest if first else rest[1:]
    f = pl.program_id(0)

    @pl.when(f == 0)
    def _():
        acc_ref[...] = jnp.zeros_like(acc_ref) if first else acc_in_ref[...]

    if len(fields) == 1:
        cur = fields[0]
    for at, field in enumerate(fields if len(fields) > 1 else []):

        @pl.when(f == at)
        def _():
            cur[...] = field[...]

    for j in range(9):
        sl = slice(j * 256, j * 256 + 256)
        pr, pi = own_ref[0, :, sl].astype(F32), own_ref[1, :, sl].astype(F32)
        qr, qi = cur[0, :, sl].astype(F32), cur[1, :, sl].astype(F32)
        rh, rl = split(qr * pr + qi * pi)
        ih, il = split(qr * pi - qi * pr)
        s = jnp.concatenate([rh, ih, rl, il], axis=0)
        r = lax.dot_general(s, tb_ref[...], (((0,), (0,)), ((), ())), preferred_element_type=F32)
        g1[sl, :] = r[:, :128] + r[:, 128:]
    for y in range(0, G, 2):
        rows = [slice((y + k) * G, (y + k + 1) * G) for k in range(2)]
        o = mid_pass(jnp.concatenate([g1[rows[k], :] for k in range(2)], axis=1), tf_ref[...])
        for k in range(2):
            g2[(y + k) * PITCH:(y + k) * PITCH + G, :] = o[k]
    for z in range(0, G, 2):
        d = jnp.concatenate([g2[pl.ds(z + k, G, stride=PITCH), :] for k in range(2)], axis=1)
        o = mid_pass(d, tf_ref[...])
        d = jnp.concatenate([o[k] * v_ref[0, z + k] for k in range(2)], axis=1)
        o = mid_pass(d, tv_ref[...])
        for k in range(2):
            g3[(z + k) * PITCH:(z + k) * PITCH + G, :] = o[k]
    for y in range(0, G, 2):
        d = jnp.concatenate([g3[pl.ds(y + k, G, stride=PITCH), :] for k in range(2)], axis=1)
        o = mid_pass(d, tv_ref[...])
        for k in range(2):
            rows = slice((y + k) * G, (y + k + 1) * G)
            gb[rows, :128], gb[rows, 128:] = split(o[k])
    for j in range(9):
        sl = slice(j * 256, j * 256 + 256)
        r = lax.dot_general(ti_ref[...], gb[sl, :], (((1,), (1,)), ((), ())), preferred_element_type=F32)
        w = r[:96] + r[96:]
        wr, wi = w[:G], w[G:]
        qr, qi = cur[0, :, sl].astype(F32), cur[1, :, sl].astype(F32)
        acc_ref[0, :, sl] += qr * wr - qi * wi
        acc_ref[1, :, sl] += qr * wi + qi * wr


def convolve(own, fields, sides, v, acc):
    constants = [jnp.asarray(t) for t in tables()]
    first = acc is None
    flat, places = [], []
    for field in fields:
        array, index = field if isinstance(field, tuple) else (field, None)
        known = [k for k, other in enumerate(flat) if other is array]
        places.append((known[0] if known else len(flat), index))
        if not known:
            flat.append(array)
    operands = [own, *flat, v, *constants] + ([] if first else [acc])
    full = lambda t: pl.BlockSpec(t.shape, lambda f: (0,) * t.ndim)
    specs = [full(t) for t in operands]
    step = sides[-1] - sides[0]
    specs[1 + len(flat)] = pl.BlockSpec((1, G, G, 128), lambda f: (sides[0] + f * step, 0, 0, 0))
    shape = jax.ShapeDtypeStruct((2, G, YZ), F32)
    return pl.pallas_call(
        functools.partial(kernel, first, tuple(places)),
        grid=(len(fields),),
        in_specs=specs,
        out_specs=full(shape),
        out_shape=shape,
        scratch_shapes=[pltpu.VMEM((2, G, YZ), BF)] + [pltpu.VMEM((YZ, 128), F32)] + [pltpu.VMEM((G * PITCH + 8, 128), F32)] * 2 + [pltpu.VMEM((YZ, 256), BF)],
        compiler_params=pltpu.CompilerParams(vmem_limit_bytes=40 << 20),
        cost_estimate=pl.CostEstimate(flops=int(1e8), bytes_accessed=1 << 16, transcendentals=0),
    )(*operands)


def coulomb_zyx(offset):
    index = jnp.arange(G, dtype=jnp.int32)
    freq = jnp.where(index < G // 2, index, index - G).astype(F32)
    lane = jnp.arange(128, dtype=jnp.int32) % 64
    fx = jnp.where(lane < G // 2, lane, lane - G).astype(F32)
    ex = (lane == G // 2) | (lane >= G)
    e = index == G // 2
    ax = (offset[0] + fx) ** 2
    ay = (offset[1] + freq) ** 2
    az = (offset[2] + freq) ** 2
    sq = ax[None, None, :] + ay[None, :, None] + az[:, None, None]
    cut = ex[None, None, :] | e[None, :, None] | e[:, None, None]
    safe = jnp.where(cut, 1.0, sq)
    return jnp.where(cut, 0.0, (G ** 1.5 / 16.0 / G ** 3) / safe)


def kpoint_coords(labels):
    first = labels % 4
    second = labels // 4 % 4
    third = labels // 16
    return jnp.stack([first, second, third], axis=1).astype(F32) / 4


def band_hop(value, by):
    n = lax.axis_size("band")
    return lax.ppermute(value, "band", [(i, (i + by) % n) for i in range(n)])


def swap_chip(value):
    n = lax.axis_size("kpool")
    return lax.ppermute(value, "kpool", [(i, i ^ 1) for i in range(n)])


def swap_next(value):
    n = lax.axis_size("kpool")
    return lax.ppermute(value, "kpool", [(i, (i + 1 if i % 2 else i - 1) % n) for i in range(n)])


def per_device(psi, kpoint_of_pool):
    own = psi[0, :, 0]
    pools = lax.axis_size("kpool")
    block = lax.axis_size("band")
    myself = lax.axis_index("kpool")
    coords = kpoint_coords(kpoint_of_pool)
    at = lambda pool: lax.dynamic_index_in_dim(coords, pool % pools, 0, keepdims=False)
    weight = -((2.0 * block) ** (-0.5))
    odd = myself % 2
    inner = myself + 1 - 2 * odd
    outer = myself - 1 + 2 * odd
    v = jnp.stack([coulomb_zyx(at(myself) - at(s)) * weight for s in (inner, outer)])
    acc = None
    outer, inner = swap_next(own), swap_chip(own)
    up, down = band_hop(own, 1), band_hop(own, -1)
    acc = convolve(own, [inner], [0], v, None)
    up, acc = lax.optimization_barrier((up, acc))
    hop_up = band_hop(up[0], 1)
    down, acc = lax.optimization_barrier((down, acc))
    across = [hop_up, band_hop(down[1], -1)]
    both = jnp.stack([up, down])
    inner, outer_both = swap_chip(both), swap_next(both)
    acc = convolve(own, [(inner, 0), (inner, 1)], [0, 0], v, acc)
    acc = convolve(own, [outer], [1], v, acc)
    across, acc = lax.optimization_barrier((across, acc))
    across = jnp.stack(across)
    inner, outer = swap_chip(across), swap_next(across)
    acc = convolve(own, [inner], [0], v, acc)
    acc = convolve(own, [(outer_both, 0), (outer_both, 1)], [1, 1], v, acc)
    acc = convolve(own, [outer], [1], v, acc)
    return acc[None, :, None]


def solution(mesh):
    in_specs = (P("kpool", None, "band", None, None), P())
    out_specs = P("kpool", None, "band", None, None)
    return jax.shard_map(per_device, mesh=mesh, in_specs=in_specs, out_specs=out_specs, check_vma=False)
```
